512 devices in a mesh: dp: 64 (over y, z), mp: 8 (over x, core).
Axes of the slice: x: 4, y: 4, z: 16, core: 2. Of those that a mesh axis runs over, the one named last changes fastest.
Arguments:
- x_proxy: bfloat16 [16384, 2048], P('dp'), may hold values from -16 to 16
- x_ref: bfloat16 [16384, 2048], P('dp'), may hold values from -6 to 6
- target: bfloat16 [16384, 2048], P('dp'), may hold values from -6 to 6
- domain: int32 [16384], P('dp'), may hold values from 0 to 21
- live_tokens: int32 [64], P('dp'), may hold values from 1 to 256, 10240 in all
- prior_counts: int32 [22], replicated, may hold values from 1 to 3
- gate_p: bfloat16 [2048, 4096], P('dp', 'mp'), may hold values from -0.125 to 0.125
- up_p: bfloat16 [2048, 4096], P('dp', 'mp'), may hold values from -0.125 to 0.125
- down_p: bfloat16 [4096, 2048], P('mp', 'dp'), may hold values from -0.1875 to 0.1875
- gate_r: bfloat16 [2048, 4096], P('dp', 'mp'), may hold values from -0.125 to 0.125
- up_r: bfloat16 [2048, 4096], P('dp', 'mp'), may hold values from -0.125 to 0.125
- down_r: bfloat16 [4096, 2048], P('mp', 'dp'), may hold values from -0.1875 to 0.1875
Outputs:
- excess: float32 [16384], P('dp')
- log_weights: float32 [22], replicated
- grad_up: float32 [2048, 4096], P('dp', 'mp')
The draws below stay inside these ranges and needn't reach their ends.
Inputs may be any that keep to these rules, and one draw needn't show every extreme that they name: `live_tokens`: one index of dp has all 256 slots live.
All inputs are finite; a program needn't handle non-finite values. No bound on the sum of `live_tokens` on one device may be relied on, other than what follows from the above.
Results may differ from the reference program's by a relative error of at most 0.035.
Values may be sent and summed in bfloat16 or wider, within the bound.
No kernel may reach another device: no remote copies, remote signals or barrier semaphores. Data moves between devices by JAX's collectives and lax.ppermute only.
A program may use at most 64 MiB of HBM per device.

```python
import math
import jax
import jax.numpy as jnp
import numpy as np
from jax import lax

D = 2048
FFW = 4096
NDOM = 22
TOK_DEV = 256
TOKENS = 16384
N_DP = 64
N_MP = 8


def set_ends(values, key, least, high):
    dims = values.shape
    place = [jax.random.randint(jax.random.fold_in(key, axis), (), 0, dims[axis]) for axis in range(len(dims))]
    values = values.at[tuple(place)].set(least)
    longest = dims.index(max(dims))
    place[longest] = (place[longest] + 1) % dims[longest]
    return values.at[tuple(place)].set(high)


def spiked(drawn, own_key, source, target, shards_of, factor):
    def block_of(position):
        return (jnp.arange(drawn.shape[position]) // (drawn.shape[position] // shards_of)).reshape((-1,) + (1,) * (drawn.ndim - 1 - position))

    one_side = jax.random.permutation(own_key, shards_of)[block_of(target)]
    other_side = (block_of(target) + shards_of // 2) % shards_of
    return jnp.where((block_of(source) == one_side) | (block_of(source) == other_side), factor * drawn, drawn)


def levels(own_key, shape, split, low, high):
    def one(dim, blocks):
        steps = jax.random.uniform(jax.random.fold_in(jax.random.fold_in(own_key, 6), dim), (blocks,), jnp.float32, low / len(split), high / len(split))
        return jnp.repeat(jnp.exp(steps), shape[dim] // blocks).reshape((-1,) + (1,) * (len(shape) - dim - 1))

    loudness = one(*split[0])
    for cut in split[1:]:
        loudness = loudness * one(*cut)
    return loudness


def cumulative_ranks(amount, lean):
    portions = [(1 << 20) // math.isqrt(standing ** lean) + 1 for standing in range(1, amount + 1)]
    spread = 1 + sum(portions) // (1 << 30)
    return np.cumsum(np.array([max(1, weight // spread) for weight in portions]))


def ranked(own_key, extent, count, slope):
    table = cumulative_ranks(count, slope)
    lot = jax.random.randint(jax.random.fold_in(own_key, 1), extent, 0, int(table[count - 1]))
    grade = jnp.searchsorted(jnp.asarray(table, jnp.int32), lot, side="right")
    return jax.random.permutation(jax.random.fold_in(own_key, 2), count)[grade].astype(jnp.int32)


def length_profile(number_of, total, most, skew):
    loads = [(1 << 20) // math.isqrt(rank ** skew) + 1 for rank in range(2, number_of + 1)]
    rest, given = total - most - (number_of - 1), [1] * (number_of - 1)
    while rest > 0:
        free = [i for i in range(number_of - 1) if given[i] < most]
        pool, budget = sum([loads[i] for i in free]), rest
        for i in free:
            addition = min(most - given[i], max(1, budget * loads[i] // pool), rest)
            given[i] = given[i] + addition
            rest = rest - addition
    return np.array([most] + given)


def uneven_parts(own_key, count, total, bound, slope):
    if count == 2:
        one = jax.random.randint(own_key, (), max(1, total - bound), min(bound, total - 1) + 1)
        return jnp.stack([one, total - one])
    tallies = jnp.asarray(length_profile(count, total, bound, slope), jnp.int32)
    couples = (count - 1) // 2
    giver, sink = tallies[1:1 + 2 * couples:2], tallies[2:2 + 2 * couples:2]
    margin = jnp.minimum(giver - 1, bound - sink)
    moved = jax.random.randint(jax.random.fold_in(own_key, 1), (couples,), 0, 1 << 20) % (margin + 1)
    tallies = tallies.at[1:1 + 2 * couples:2].set(giver - moved).at[2:2 + 2 * couples:2].set(sink + moved)
    return tallies[jax.random.permutation(jax.random.fold_in(own_key, 2), count)]


def noise(stream_key, shape, scale, limit, pieces=(), kind=jnp.bfloat16):
    gain = levels(stream_key, shape, pieces, -0.22, 0.18) if pieces else 1.0
    values = jax.random.normal(stream_key, shape, jnp.float32) * scale * gain
    return jnp.minimum(jnp.maximum(values, -limit), limit).astype(kind)


def heavy_noise(rng, extent, deviation, limit, split, heavy, held_as=jnp.bfloat16):
    result = deviation * jax.random.normal(rng, extent, jnp.float32)
    if split:
        result = result * levels(rng, extent, split, -0.22, 0.18)
    return jnp.clip(spiked(result, jax.random.fold_in(rng, 3), *heavy), -limit, limit).astype(held_as)


def setup_inputs(seed: int = 0) -> dict:
    arg_keys = jax.random.split(jax.random.key(seed), 13)
    return {
        "x_proxy": heavy_noise(arg_keys[0], (TOKENS, D), 1.0, 16.0, ((0, 64),), (0, 1, 64, 4.0)),
        "x_ref": noise(arg_keys[1], (TOKENS, D), 1.0, 6.0, ((0, 64),)),
        "target": noise(arg_keys[2], (TOKENS, D), 1.0, 6.0, ((0, 64),)),
        "domain": set_ends(ranked(arg_keys[3], (TOKENS,), NDOM, 2), jax.random.fold_in(arg_keys[3], 3), 0, NDOM - 1).astype(jnp.int32),
        "live_tokens": uneven_parts(arg_keys[4], N_DP, TOKENS * 5 // 8, TOK_DEV, 2).astype(jnp.int32),
        "prior_counts": set_ends(jax.random.randint(arg_keys[5], (NDOM,), 1, 4), jax.random.fold_in(arg_keys[5], 1), 1, 3).astype(jnp.int32),
        "gate_p": noise(arg_keys[6], (D, FFW), D ** -0.5, 0.125, ((0, 64), (1, 8))),
        "up_p": noise(arg_keys[7], (D, FFW), D ** -0.5, 0.125, ((0, 64), (1, 8))),
        "down_p": noise(arg_keys[8], (FFW, D), (FFW // 4) ** -0.5, 0.1875, ((0, 8), (1, 64))),
        "gate_r": noise(arg_keys[9], (D, FFW), D ** -0.5, 0.125, ((0, 64), (1, 8))),
        "up_r": noise(arg_keys[10], (D, FFW), D ** -0.5, 0.125, ((0, 64), (1, 8))),
        "down_r": noise(arg_keys[11], (FFW, D), (FFW // 4) ** -0.5, 0.1875, ((0, 8), (1, 64))),
    }


def layer_out(x, gate_w, up_w, down_w):
    gate = jnp.dot(x, gate_w, preferred_element_type=jnp.float32)
    up = jnp.dot(x, up_w, preferred_element_type=jnp.float32)
    hid = (jax.nn.silu(gate) * up).astype(jnp.bfloat16)
    block = math.gcd(TOKENS, 512)
    blocks = hid.reshape(TOKENS // block, block, N_MP, FFW // N_MP)
    down_blocks = down_w.reshape(N_MP, FFW // N_MP, D).astype(jnp.float32)

    def one_block(piece):
        parts = jnp.einsum("tmf,mfd->tmd", piece.astype(jnp.float32), down_blocks)
        return jnp.sum(parts.astype(jnp.bfloat16).astype(jnp.float32), axis=1)

    summed = lax.map(one_block, blocks).reshape(TOKENS, D)
    return x.astype(jnp.float32) + summed, gate


def reference(x_proxy, x_ref, target, domain, live_tokens, prior_counts, gate_p, up_p, down_p, gate_r, up_r, down_r):
    out_p, gate_proxy = layer_out(x_proxy, gate_p, up_p, down_p)
    out_r, gate_other = layer_out(x_ref, gate_r, up_r, down_r)
    goal = target.astype(jnp.float32)
    loss_p = jnp.mean((out_p - goal) ** 2, axis=1)
    loss_r = jnp.mean((out_r - goal) ** 2, axis=1)
    positions = jnp.arange(TOKENS, dtype=jnp.int32)
    owner = (positions // TOK_DEV).astype(jnp.int32)
    live = ((positions % TOK_DEV) < live_tokens[owner]).astype(jnp.float32)
    excess = live * jnp.maximum(loss_p - loss_r, 0.0)
    onehot = (domain[:, None] == jnp.arange(NDOM, dtype=jnp.int32)[None, :]).astype(jnp.float32)
    dsum = jnp.sum(onehot * excess[:, None], axis=0)
    count = jnp.sum(onehot * live[:, None], axis=0)
    raw = prior_counts.astype(jnp.float32) * jnp.exp(1.0 * dsum / (count + 1.0))
    alpha = (1.0 - 0.001) * raw / jnp.sum(raw) + 0.001 / NDOM
    log_weights = jnp.log(alpha)
    table = alpha * TOKENS / (count + 1.0)
    weight_tok = live * table[domain]
    dout = (weight_tok[:, None] * 2.0 * (out_p - goal) / D).astype(jnp.bfloat16)
    dhid = jnp.dot(dout, down_p.T, preferred_element_type=jnp.float32)
    dup = (dhid * jax.nn.silu(gate_proxy)).astype(jnp.bfloat16)
    grad_up = jnp.dot(x_proxy.T, dup, preferred_element_type=jnp.float32)
    return excess, log_weights, grad_up
```

```python
import jax
import jax.numpy as jnp
from jax import lax
from jax.sharding import Mesh
from jax.sharding import PartitionSpec as P

NDOM = 22
LANES = 128
BF16 = jnp.bfloat16
F32 = jnp.float32
DP = ("y", "z")
MP = ("x", "c")


def dot(a, b, dims):
    return lax.dot_general(a, b, (dims, ((), ())), preferred_element_type=F32)


def exchange(value, axis):
    return lax.all_to_all(value, axis, 0, 0, tiled=True)


def gather(value, axis):
    return lax.all_gather(value, axis, axis=0, tiled=True)


def column_parts(x, parts):
    rows, width = x.shape
    return x.reshape(rows, parts, width // parts).transpose(1, 0, 2)


def body(
    x_proxy,
    x_ref,
    target,
    domain,
    live_tokens,
    prior_counts,
    gate_p,
    up_p,
    down_p,
    gate_r,
    up_r,
    down_r,
):
    rows, width = x_proxy.shape
    hidden = gate_p.shape[1]
    n_y, n_z = lax.axis_size("y"), lax.axis_size("z")
    n_dp, n_mp = n_y * n_z, lax.axis_size(MP)
    total_rows = rows * n_dp
    share = rows // n_mp
    me = lax.axis_index(MP)

    packed = jnp.concatenate([gate_p, up_p, gate_r, up_r, down_p.T, down_r.T], axis=1)
    held = gather(packed, "z")
    down = gather(held[:, 4 * hidden :], "y")
    down_of_p, down_of_r = down[:, :hidden], down[:, hidden:]

    sliced_p = exchange(column_parts(x_proxy, n_y), "y").reshape(n_y * rows, -1)
    sliced_r = exchange(column_parts(x_ref, n_y), "y").reshape(n_y * rows, -1)

    slots = jnp.arange(rows, dtype=jnp.int32)
    alive = slots < live_tokens[0]
    live = alive.astype(F32)
    group = gather(jnp.where(alive, domain, NDOM), "y")

    def layer(sliced, weights, down_w):
        partial = dot(sliced, weights, ((1,), (0,))).astype(BF16)
        both = exchange(partial.reshape(n_y, rows, 2 * hidden), "y").astype(F32).sum(axis=0)
        act = jax.nn.silu(both[:, :hidden])
        hid = (act * both[:, hidden:]).astype(BF16)
        part = dot(hid, down_w, ((1,), (1,))).astype(BF16)
        terms = exchange(part.reshape(n_mp, share, width), MP)
        return act, terms.astype(F32).sum(axis=0)

    def own(x):
        return lax.dynamic_slice_in_dim(x, me * share, share, axis=0).astype(F32)

    goal = own(target)
    act_p, summed_p = layer(sliced_p, held[:, : 2 * hidden], down_of_p)
    diff_p = own(x_proxy) + summed_p - goal
    loss_p = jnp.mean(diff_p**2, axis=1)
    diff_all = gather(diff_p.astype(BF16), MP)

    _, summed_r = layer(sliced_r, held[:, 2 * hidden : 4 * hidden], down_of_r)
    diff_r = own(x_ref) + summed_r - goal
    loss_r = jnp.mean(diff_r**2, axis=1)

    dhid = dot(diff_all, down_of_p, ((1,), (0,)))
    scaled = gather((dhid * act_p * (2.0 / width)).astype(BF16), "y")

    excess = live * gather(jnp.maximum(loss_p - loss_r, 0.0), MP)
    onehot = (domain[:, None] == jnp.arange(NDOM, dtype=jnp.int32)[None, :]).astype(F32)
    sums = jnp.concatenate(
        [jnp.sum(onehot * excess[:, None], axis=0), jnp.sum(onehot * live[:, None], axis=0)]
    )
    sums = jnp.pad(sums, (0, LANES - 2 * NDOM))
    sums = exchange(jnp.broadcast_to(sums[None, :], (n_dp, LANES)), DP).sum(axis=0)
    dsum, count = sums[:NDOM], sums[NDOM : 2 * NDOM]
    raw = prior_counts.astype(F32) * jnp.exp(1.0 * dsum / (count + 1.0))
    alpha = (1.0 - 0.001) * raw / jnp.sum(raw) + 0.001 / NDOM
    log_weights = jnp.log(alpha)
    table = alpha * total_rows / (count + 1.0)

    picks = (group[:, None] == jnp.arange(NDOM, dtype=jnp.int32)[None, :]).astype(F32)
    weight_tok = jnp.sum(picks * table[None, :], axis=1)
    dup = (scaled.astype(F32) * weight_tok[:, None]).astype(BF16)
    grad = dot(sliced_p, dup, ((0,), (0,))).astype(BF16)
    grad_up = exchange(grad.reshape(n_z, -1, hidden), "z").astype(F32).sum(axis=0)
    return (excess, log_weights, grad_up)


def solution(mesh):
    fine = Mesh(mesh.devices.reshape(4, 16, 4, 2), DP + MP)
    tokens, weights = P(DP, None), P(DP, MP)
    in_specs = (
        tokens,
        tokens,
        tokens,
        P(DP),
        P(DP),
        P(),
        weights,
        weights,
        P(MP, DP),
        weights,
        weights,
        P(MP, DP),
    )
    out_specs = (P(DP), P(), weights)
    return jax.shard_map(body, mesh=fine, in_specs=in_specs, out_specs=out_specs, check_vma=False)
```

```python
import jax
import jax.numpy as jnp
from jax import lax
from jax.sharding import Mesh
from jax.sharding import PartitionSpec as P

NDOM = 22
LANES = 128
BF16 = jnp.bfloat16
F32 = jnp.float32
DP = ("y", "z")
MP = ("x", "c")


def dot(a, b, dims):
    return lax.dot_general(a, b, (dims, ((), ())), preferred_element_type=F32)


def exchange(value, axis):
    return lax.all_to_all(value, axis, 0, 0, tiled=True)


def gather(value, axis):
    return lax.all_gather(value, axis, axis=0, tiled=True)


def share_all(value, axis):
    copies = jnp.broadcast_to(value[None], (lax.axis_size(axis),) + value.shape)
    return lax.all_to_all(copies, axis, 0, 0, tiled=True)


def after(*values):
    return lax.optimization_barrier(values)


def column_parts(x, parts):
    rows, width = x.shape
    return x.reshape(rows, parts, width // parts).transpose(1, 0, 2)


def body(
    x_proxy,
    x_ref,
    target,
    domain,
    live_tokens,
    prior_counts,
    gate_p,
    up_p,
    down_p,
    gate_r,
    up_r,
    down_r,
):
    rows, width = x_proxy.shape
    hidden = gate_p.shape[1]
    n_y, n_z = lax.axis_size("y"), lax.axis_size("z")
    n_dp, n_mp = n_y * n_z, lax.axis_size(MP)
    total_rows = rows * n_dp
    share = rows // n_mp
    me = lax.axis_index(MP)

    packed = jnp.concatenate([gate_p, up_p, gate_r, up_r, down_r.T], axis=1)
    packed, whole_p, whole_r = after(packed, x_proxy, x_ref)
    held = gather(packed, "z")

    parts = jnp.stack([column_parts(whole_p, n_y), column_parts(whole_r, n_y)], axis=1)
    sliced = exchange(parts, "y")
    sliced_p = sliced[:, 0].reshape(n_y * rows, -1)
    sliced_r = sliced[:, 1].reshape(n_y * rows, -1)

    slots = jnp.arange(rows, dtype=jnp.int32)
    alive = slots < live_tokens[0]
    live = alive.astype(F32)
    down_of_p, group = after(gather(down_p.T, "z"), jnp.where(alive, domain, NDOM))
    down_of_p = share_all(down_of_p, "y").reshape(width, hidden)
    group = gather(group, "y")
    held, sliced_p, sliced_r, group, down_of_p = after(held, sliced_p, sliced_r, group, down_of_p)
    down_of_r = gather(held[:, 4 * hidden :], "y")

    def first(sliced, weights):
        partial = dot(sliced, weights, ((1,), (0,))).astype(BF16)
        return partial.reshape(n_y, rows, 2 * hidden)

    def halves(terms):
        both = terms.astype(F32).sum(axis=0)
        act = jax.nn.silu(both[:, :hidden])
        return act, (act * both[:, hidden:]).astype(BF16)

    def second(hid, down_w):
        part = dot(hid, down_w, ((1,), (1,))).astype(BF16)
        return part.reshape(n_mp, share, width)

    def own(x):
        return lax.dynamic_slice_in_dim(x, me * share, share, axis=0).astype(F32)

    goal = own(target)
    terms_p = exchange(first(sliced_p, held[:, : 2 * hidden]), "y")
    partial_r = first(sliced_r, held[:, 2 * hidden : 4 * hidden])
    terms_p, partial_r = after(terms_p, partial_r)
    terms_r = exchange(partial_r, "y")

    act_p, hid_p = halves(terms_p)
    summed_p = exchange(second(hid_p, down_of_p), MP).astype(F32).sum(axis=0)
    diff_p = own(x_proxy) + summed_p - goal
    loss_p = jnp.mean(diff_p**2, axis=1)
    diff_low = diff_p.astype(BF16)

    _, hid_r = halves(terms_r)
    parts_r = exchange(second(hid_r, down_of_r), MP)
    diff_all = gather(diff_low, MP)
    loss_p, parts_r = after(loss_p, parts_r)
    diff_r = own(x_ref) + parts_r.astype(F32).sum(axis=0) - goal
    loss_r = jnp.mean(diff_r**2, axis=1)

    dhid = dot(diff_all, down_of_p, ((1,), (0,)))
    scaled = gather((dhid * act_p * (2.0 / width)).astype(BF16), "y")

    live_own = lax.dynamic_slice_in_dim(live, me * share, share, axis=0)
    domain_own = lax.dynamic_slice_in_dim(domain, me * share, share, axis=0)
    gained = live_own * jnp.maximum(loss_p - loss_r, 0.0)
    ids = jnp.arange(NDOM, dtype=jnp.int32)[None, :]
    onehot = (domain_own[:, None] == ids).astype(F32)
    sums = jnp.concatenate(
        [jnp.sum(onehot * gained[:, None], axis=0), jnp.sum(onehot * live_own[:, None], axis=0)]
    )
    sums = jnp.pad(sums, (0, LANES - 2 * NDOM))
    sums = share_all(sums, "z").sum(axis=0)
    sums = share_all(sums, ("y",) + MP).sum(axis=0)
    dsum, count = sums[:NDOM], sums[NDOM : 2 * NDOM]
    raw = prior_counts.astype(F32) * jnp.exp(1.0 * dsum / (count + 1.0))
    alpha = (1.0 - 0.001) * raw / jnp.sum(raw) + 0.001 / NDOM
    log_weights = jnp.log(alpha)
    table = alpha * total_rows / (count + 1.0)

    picks = (group[:, None] == ids).astype(F32)
    weight_tok = jnp.sum(picks * table[None, :], axis=1)
    dup = (scaled.astype(F32) * weight_tok[:, None]).astype(BF16)
    grad = dot(sliced_p, dup, ((0,), (0,))).astype(BF16)
    grad, gained = after(grad, gained)
    grad_up = exchange(grad.reshape(n_z, -1, hidden), "z").astype(F32).sum(axis=0)
    excess = gather(gained, MP)
    return (excess, log_weights, grad_up)


def solution(mesh):
    fine = Mesh(mesh.devices.reshape(4, 16, 4, 2), DP + MP)
    tokens, weights = P(DP, None), P(DP, MP)
    in_specs = (
        tokens,
        tokens,
        tokens,
        P(DP),
        P(DP),
        P(),
        weights,
        weights,
        P(MP, DP),
        weights,
        weights,
        P(MP, DP),
    )
    out_specs = (P(DP), P(), weights)
    return jax.shard_map(body, mesh=fine, in_specs=in_specs, out_specs=out_specs, check_vma=False)
```

```python
import jax
import jax.numpy as jnp
from jax import lax
from jax.sharding import Mesh
from jax.sharding import PartitionSpec as P

NDOM = 22
LANES = 128
BF16 = jnp.bfloat16
F32 = jnp.float32
DP = ("y", "z")
MP = ("x", "c")


def dot(a, b, dims):
    return lax.dot_general(a, b, (dims, ((), ())), preferred_element_type=F32)


def exchange(value, axis):
    return lax.all_to_all(value, axis, 0, 0, tiled=True)


def gather(value, axis):
    return lax.all_gather(value, axis, axis=0, tiled=True)


def share_all(value, axis):
    copies = jnp.broadcast_to(value[None], (lax.axis_size(axis),) + value.shape)
    return lax.all_to_all(copies, axis, 0, 0, tiled=True)


def sent_round(value, axis):
    n = lax.axis_size(axis)
    sends = [[(i, (i + k) % n) for i in range(n)] for k in range(1, n)]
    return [value] + [lax.ppermute(value, axis, perm) for perm in sends]


def turned(blocks, axis):
    n, i = lax.axis_size(axis), lax.axis_index(axis)
    return jnp.stack([blocks[(i + n - k) % n] for k in range(n)])


def sum_of_shares(shares):
    n_x, n_c = lax.axis_size("x"), lax.axis_size("c")
    x, c = lax.axis_index("x"), lax.axis_index("c")
    shares = shares.reshape((n_x, n_c) + shares.shape[1:])
    keep = lax.dynamic_index_in_dim(shares, c, 1, keepdims=False)
    give = lax.dynamic_index_in_dim(shares, (c + 1) % n_c, 1, keepdims=False)
    got = lax.ppermute(give, "c", [(i, (i + 1) % n_c) for i in range(n_c)])
    pair = keep.astype(F32) + got.astype(F32)
    low = pair.astype(BF16)
    total = lax.dynamic_index_in_dim(pair, x, 0, keepdims=False)
    for k in range(1, n_x):
        block = lax.dynamic_index_in_dim(low, (x + k) % n_x, 0, keepdims=False)
        perm = [(i, (i + k) % n_x) for i in range(n_x)]
        total = total + lax.ppermute(block, "x", perm).astype(F32)
    return total


def after(*values):
    return lax.optimization_barrier(values)


def column_parts(x, parts):
    rows, width = x.shape
    return x.reshape(rows, parts, width // parts).transpose(1, 0, 2)


def body(
    x_proxy,
    x_ref,
    target,
    domain,
    live_tokens,
    prior_counts,
    gate_p,
    up_p,
    down_p,
    gate_r,
    up_r,
    down_r,
):
    rows, width = x_proxy.shape
    hidden = gate_p.shape[1]
    n_y, n_z = lax.axis_size("y"), lax.axis_size("z")
    n_dp, n_mp = n_y * n_z, lax.axis_size(MP)
    total_rows = rows * n_dp
    share = rows // n_mp
    me = lax.axis_index(MP)

    packed = jnp.concatenate([gate_p, up_p, gate_r, up_r, down_r.T], axis=1)
    packed, whole_p, whole_r = after(packed, x_proxy, x_ref)
    held = gather(packed, "z")

    parts = jnp.stack([column_parts(whole_p, n_y), column_parts(whole_r, n_y)], axis=1)
    sliced = exchange(parts, "y")
    sliced_p = sliced[:, 0].reshape(n_y * rows, -1)
    sliced_r = sliced[:, 1].reshape(n_y * rows, -1)
    turned_p = turned(sliced[:, 0], "y").reshape(n_y * rows, -1)

    slots = jnp.arange(rows, dtype=jnp.int32)
    alive = slots < live_tokens[0]
    live = alive.astype(F32)
    down_of_p = share_all(gather(down_p.T, "z"), "y").reshape(width, hidden)
    held, sliced_p, sliced_r, down_of_p = after(held, sliced_p, sliced_r, down_of_p)
    down_of_r = gather(held[:, 4 * hidden :], "y")

    def first(sliced, weights):
        partial = dot(sliced, weights, ((1,), (0,))).astype(BF16)
        return partial.reshape(n_y, rows, 2 * hidden)

    def halves(terms):
        both = terms.astype(F32).sum(axis=0)
        act = jax.nn.silu(both[:, :hidden])
        return act, (act * both[:, hidden:]).astype(BF16)

    def second(hid, down_w):
        part = dot(hid, down_w, ((1,), (1,))).astype(BF16)
        return part.reshape(n_mp, share, width)

    def own(x):
        return lax.dynamic_slice_in_dim(x, me * share, share, axis=0).astype(F32)

    goal = own(target)
    terms_p = exchange(first(sliced_p, held[:, : 2 * hidden]), "y")
    partial_r = first(sliced_r, held[:, 2 * hidden : 4 * hidden])
    terms_p, partial_r, group = after(terms_p, partial_r, jnp.where(alive, domain, NDOM))
    terms_r = exchange(partial_r, "y")
    group = gather(group, "y").reshape(n_y, rows)

    act_p, hid_p = halves(terms_p)
    summed_p = sum_of_shares(second(hid_p, down_of_p))
    diff_p = own(x_proxy) + summed_p - goal
    loss_p = jnp.mean(diff_p**2, axis=1)
    diff_low = diff_p.astype(BF16)

    terms_r, diff_low, loss_p, group = after(terms_r, diff_low, loss_p, group)
    _, hid_r = halves(terms_r)
    parts_r = exchange(second(hid_r, down_of_r), MP)
    diff_all = gather(diff_low, MP)
    diff_r = own(x_ref) + parts_r.astype(F32).sum(axis=0) - goal
    loss_r = jnp.mean(diff_r**2, axis=1)

    dhid = dot(diff_all, down_of_p, ((1,), (0,)))
    unweighted = (dhid * act_p * (2.0 / width)).astype(BF16)

    live_own = lax.dynamic_slice_in_dim(live, me * share, share, axis=0)
    domain_own = lax.dynamic_slice_in_dim(domain, me * share, share, axis=0)
    gained = live_own * jnp.maximum(loss_p - loss_r, 0.0)
    ids = jnp.arange(NDOM, dtype=jnp.int32)[None, :]
    onehot = (domain_own[:, None] == ids).astype(F32)
    sums = jnp.concatenate(
        [jnp.sum(onehot * gained[:, None], axis=0), jnp.sum(onehot * live_own[:, None], axis=0)]
    )
    sums = jnp.pad(sums, (0, LANES - 2 * NDOM))
    sums = share_all(sums, "z").sum(axis=0)
    sums, unweighted = after(sums, unweighted)
    scaled = sent_round(unweighted, "y")
    sums = share_all(sums, ("y",) + MP).sum(axis=0)
    dsum, count = sums[:NDOM], sums[NDOM : 2 * NDOM]
    raw = prior_counts.astype(F32) * jnp.exp(1.0 * dsum / (count + 1.0))
    alpha = (1.0 - 0.001) * raw / jnp.sum(raw) + 0.001 / NDOM
    log_weights = jnp.log(alpha)
    table = alpha * total_rows / (count + 1.0)

    picks = (turned(group, "y").reshape(-1)[:, None] == ids).astype(F32)
    weight_tok = jnp.sum(picks * table[None, :], axis=1).reshape(n_y, rows, 1)
    dup = [(block.astype(F32) * weight_tok[k]).astype(BF16) for k, block in enumerate(scaled)]
    grad = dot(turned_p, jnp.concatenate(dup, axis=0), ((0,), (0,))).astype(BF16)
    grad, gained = after(grad, gained)
    grad_up = exchange(grad.reshape(n_z, -1, hidden), "z").astype(F32).sum(axis=0)
    excess = gather(gained, MP)
    return (excess, log_weights, grad_up)


def solution(mesh):
    fine = Mesh(mesh.devices.reshape(4, 16, 4, 2), DP + MP)
    tokens, weights = P(DP, None), P(DP, MP)
    in_specs = (
        tokens,
        tokens,
        tokens,
        P(DP),
        P(DP),
        P(),
        weights,
        weights,
        P(MP, DP),
        weights,
        weights,
        P(MP, DP),
    )
    out_specs = (P(DP), P(), weights)
    return jax.shard_map(body, mesh=fine, in_specs=in_specs, out_specs=out_specs, check_vma=False)
```

```python
import jax
import jax.numpy as jnp
from jax import lax
from jax.sharding import Mesh
from jax.sharding import PartitionSpec as P

NDOM = 22
LANES = 128
BF16 = jnp.bfloat16
F32 = jnp.float32
DP = ("y", "z")
MP = ("x", "c")


def dot(a, b, dims):
    return lax.dot_general(a, b, (dims, ((), ())), preferred_element_type=F32)


def exchange(value, axis):
    return lax.all_to_all(value, axis, 0, 0, tiled=True)


def gather(value, axis):
    return lax.all_gather(value, axis, axis=0, tiled=True)


def share_all(value, axis):
    copies = jnp.broadcast_to(value[None], (lax.axis_size(axis),) + value.shape)
    return lax.all_to_all(copies, axis, 0, 0, tiled=True)


def sent_round(value, axis):
    n = lax.axis_size(axis)
    sends = [[(i, (i + k) % n) for i in range(n)] for k in range(1, n)]
    return [value] + [lax.ppermute(value, axis, perm) for perm in sends]


def turned(blocks, axis):
    n, i = lax.axis_size(axis), lax.axis_index(axis)
    return jnp.stack([blocks[(i + n - k) % n] for k in range(n)])


def sum_of_shares(shares):
    n_x, n_c = lax.axis_size("x"), lax.axis_size("c")
    x, c = lax.axis_index("x"), lax.axis_index("c")
    shares = shares.reshape((n_x, n_c) + shares.shape[1:])
    keep = lax.dynamic_index_in_dim(shares, c, 1, keepdims=False)
    give = lax.dynamic_index_in_dim(shares, (c + 1) % n_c, 1, keepdims=False)
    got = lax.ppermute(give, "c", [(i, (i + 1) % n_c) for i in range(n_c)])
    pair = keep.astype(F32) + got.astype(F32)
    low = pair.astype(BF16)
    total = lax.dynamic_index_in_dim(pair, x, 0, keepdims=False)
    for k in range(1, n_x):
        block = lax.dynamic_index_in_dim(low, (x + k) % n_x, 0, keepdims=False)
        perm = [(i, (i + k) % n_x) for i in range(n_x)]
        total = total + lax.ppermute(block, "x", perm).astype(F32)
    return total


def after(*values):
    return lax.optimization_barrier(values)


def column_parts(x, parts):
    rows, width = x.shape
    return x.reshape(rows, parts, width // parts).transpose(1, 0, 2)


def body(
    x_proxy,
    x_ref,
    target,
    domain,
    live_tokens,
    prior_counts,
    gate_p,
    up_p,
    down_p,
    gate_r,
    up_r,
    down_r,
):
    rows, width = x_proxy.shape
    hidden = gate_p.shape[1]
    n_y, n_z = lax.axis_size("y"), lax.axis_size("z")
    n_dp, n_mp = n_y * n_z, lax.axis_size(MP)
    total_rows = rows * n_dp
    share = rows // n_mp
    me = lax.axis_index(MP)

    packed = jnp.concatenate([gate_p, up_p, gate_r, up_r, down_r.T], axis=1)
    packed, whole_p, whole_r = after(packed, x_proxy, x_ref)
    held = gather(packed, "z")

    parts = jnp.stack([column_parts(whole_p, n_y), column_parts(whole_r, n_y)], axis=1)
    sliced = exchange(parts, "y")
    sliced_p = sliced[:, 0].reshape(n_y * rows, -1)
    sliced_r = sliced[:, 1].reshape(n_y * rows, -1)
    turned_p = turned(sliced[:, 0], "y").reshape(n_y * rows, -1)

    slots = jnp.arange(rows, dtype=jnp.int32)
    alive = slots < live_tokens[0]
    live = alive.astype(F32)
    down_of_p = share_all(gather(down_p.T, "z"), "y").reshape(width, hidden)
    held, sliced_p, sliced_r, down_of_p = after(held, sliced_p, sliced_r, down_of_p)
    down_of_r = gather(held[:, 4 * hidden :], "y")

    def first(sliced, weights):
        partial = dot(sliced, weights, ((1,), (0,))).astype(BF16)
        return partial.reshape(n_y, rows, 2 * hidden)

    def halves(terms):
        both = terms.astype(F32).sum(axis=0)
        act = jax.nn.silu(both[:, :hidden])
        return act, (act * both[:, hidden:]).astype(BF16)

    def second(hid, down_w):
        part = dot(hid, down_w, ((1,), (1,))).astype(BF16)
        return part.reshape(n_mp, share, width)

    def own(x):
        return lax.dynamic_slice_in_dim(x, me * share, share, axis=0).astype(F32)

    goal = own(target)
    terms_p = exchange(first(sliced_p, held[:, : 2 * hidden]), "y")
    partial_r = first(sliced_r, held[:, 2 * hidden : 4 * hidden])
    terms_p, partial_r = after(terms_p, partial_r)
    terms_r = exchange(partial_r, "y")

    act_p, hid_p = halves(terms_p)
    summed_p = sum_of_shares(second(hid_p, down_of_p))
    diff_p = own(x_proxy) + summed_p - goal
    loss_p = jnp.mean(diff_p**2, axis=1)
    diff_low = diff_p.astype(BF16)

    terms_r, diff_low, loss_p, group = after(
        terms_r, diff_low, loss_p, jnp.where(alive, domain, NDOM)
    )
    _, hid_r = halves(terms_r)
    group = gather(group, "y").reshape(n_y, rows)
    parts_r = exchange(second(hid_r, down_of_r), MP)
    parts_r, group = after(parts_r, group)
    diff_all = gather(diff_low, MP)
    diff_r = own(x_ref) + parts_r.astype(F32).sum(axis=0) - goal
    loss_r = jnp.mean(diff_r**2, axis=1)

    dhid = dot(diff_all, down_of_p, ((1,), (0,)))
    unweighted = (dhid * act_p * (2.0 / width)).astype(BF16)

    live_own = lax.dynamic_slice_in_dim(live, me * share, share, axis=0)
    domain_own = lax.dynamic_slice_in_dim(domain, me * share, share, axis=0)
    gained = live_own * jnp.maximum(loss_p - loss_r, 0.0)
    ids = jnp.arange(NDOM, dtype=jnp.int32)[None, :]
    onehot = (domain_own[:, None] == ids).astype(F32)
    sums = jnp.concatenate(
        [jnp.sum(onehot * gained[:, None], axis=0), jnp.sum(onehot * live_own[:, None], axis=0)]
    )
    sums = jnp.pad(sums, (0, LANES - 2 * NDOM))
    sums = share_all(sums, "z").sum(axis=0)
    sums, unweighted = after(sums, unweighted)
    scaled = sent_round(unweighted, "y")
    sums = share_all(sums, ("y",) + MP).sum(axis=0)
    dsum, count = sums[:NDOM], sums[NDOM : 2 * NDOM]
    raw = prior_counts.astype(F32) * jnp.exp(1.0 * dsum / (count + 1.0))
    alpha = (1.0 - 0.001) * raw / jnp.sum(raw) + 0.001 / NDOM
    log_weights = jnp.log(alpha)
    table = alpha * total_rows / (count + 1.0)

    picks = (turned(group, "y").reshape(-1)[:, None] == ids).astype(F32)
    weight_tok = jnp.sum(picks * table[None, :], axis=1).reshape(n_y, rows, 1)
    dup = [(block.astype(F32) * weight_tok[k]).astype(BF16) for k, block in enumerate(scaled)]
    grad = dot(turned_p, jnp.concatenate(dup, axis=0), ((0,), (0,))).astype(BF16)
    grad, gained = after(grad, gained)
    grad_up = exchange(grad.reshape(n_z, -1, hidden), "z").astype(F32).sum(axis=0)
    excess = gather(gained, MP)
    return (excess, log_weights, grad_up)


def solution(mesh):
    fine = Mesh(mesh.devices.reshape(4, 16, 4, 2), DP + MP)
    tokens, weights = P(DP, None), P(DP, MP)
    in_specs = (
        tokens,
        tokens,
        tokens,
        P(DP),
        P(DP),
        P(),
        weights,
        weights,
        P(MP, DP),
        weights,
        weights,
        P(MP, DP),
    )
    out_specs = (P(DP), P(), weights)
    return jax.shard_map(body, mesh=fine, in_specs=in_specs, out_specs=out_specs, check_vma=False)
```

```python
import jax
import jax.numpy as jnp
from jax import lax
from jax.sharding import Mesh
from jax.sharding import PartitionSpec as P

NDOM = 22
LANES = 128
BF16 = jnp.bfloat16
F32 = jnp.float32
DP = ("y", "z")
MP = ("x", "c")


def dot(a, b, dims):
    return lax.dot_general(a, b, (dims, ((), ())), preferred_element_type=F32)


def exchange(value, axis):
    return lax.all_to_all(value, axis, 0, 0, tiled=True)


def gather(value, axis):
    return lax.all_gather(value, axis, axis=0, tiled=True)


def share_all(value, axis):
    copies = jnp.broadcast_to(value[None], (lax.axis_size(axis),) + value.shape)
    return lax.all_to_all(copies, axis, 0, 0, tiled=True)


def sum_of_shares(shares):
    n_x, n_c = lax.axis_size("x"), lax.axis_size("c")
    x, c = lax.axis_index("x"), lax.axis_index("c")
    shares = shares.reshape((n_x, n_c) + shares.shape[1:])
    keep = lax.dynamic_index_in_dim(shares, c, 1, keepdims=False)
    give = lax.dynamic_index_in_dim(shares, (c + 1) % n_c, 1, keepdims=False)
    got = lax.ppermute(give, "c", [(i, (i + 1) % n_c) for i in range(n_c)])
    pair = keep.astype(F32) + got.astype(F32)
    low = pair.astype(BF16)
    total = lax.dynamic_index_in_dim(pair, x, 0, keepdims=False)
    for k in range(1, n_x):
        block = lax.dynamic_index_in_dim(low, (x + k) % n_x, 0, keepdims=False)
        perm = [(i, (i + k) % n_x) for i in range(n_x)]
        total = total + lax.ppermute(block, "x", perm).astype(F32)
    return total


def after(*values):
    return lax.optimization_barrier(values)


def column_parts(x, parts):
    rows, width = x.shape
    return x.reshape(rows, parts, width // parts).transpose(1, 0, 2)


def body(
    x_proxy,
    x_ref,
    target,
    domain,
    live_tokens,
    prior_counts,
    gate_p,
    up_p,
    down_p,
    gate_r,
    up_r,
    down_r,
):
    rows, width = x_proxy.shape
    hidden = gate_p.shape[1]
    n_y, n_z = lax.axis_size("y"), lax.axis_size("z")
    n_dp, n_mp = n_y * n_z, lax.axis_size(MP)
    total_rows = rows * n_dp
    share = rows // n_mp
    me = lax.axis_index(MP)

    packed = jnp.concatenate([gate_p, up_p, gate_r, up_r], axis=1)
    packed, whole_p, whole_r = after(packed, x_proxy, x_ref)
    held = gather(packed, "z")

    parts = jnp.stack([column_parts(whole_p, n_y), column_parts(whole_r, n_y)], axis=1)
    sliced = exchange(parts, "y")
    sliced_p = sliced[:, 0].reshape(n_y * rows, -1)
    sliced_r = sliced[:, 1].reshape(n_y * rows, -1)

    slots = jnp.arange(rows, dtype=jnp.int32)
    alive = slots < live_tokens[0]
    live = alive.astype(F32)
    down_of_p, down_of_r = after(gather(down_p.T, "z"), down_r.T)
    down_of_p = share_all(down_of_p, "y").reshape(width, hidden)
    down_of_r = gather(down_of_r, "y")
    held, sliced_p, sliced_r, down_of_r = after(held, sliced_p, sliced_r, down_of_r)
    down_of_r = gather(down_of_r, "z").reshape(n_z, n_y, -1, hidden)
    down_of_r = down_of_r.transpose(1, 0, 2, 3).reshape(width, hidden)

    def first(sliced, weights):
        partial = dot(sliced, weights, ((1,), (0,))).astype(BF16)
        return partial.reshape(n_y, rows, 2 * hidden)

    def halves(terms):
        both = terms.astype(F32).sum(axis=0)
        act = jax.nn.silu(both[:, :hidden])
        return act, (act * both[:, hidden:]).astype(BF16)

    def second(hid, down_w):
        part = dot(hid, down_w, ((1,), (1,))).astype(BF16)
        return part.reshape(n_mp, share, width)

    def own(x):
        return lax.dynamic_slice_in_dim(x, me * share, share, axis=0).astype(F32)

    goal = own(target)
    partial_p, down_of_p = after(first(sliced_p, held[:, : 2 * hidden]), down_of_p)
    terms_p = exchange(partial_p, "y")
    partial_r = first(sliced_r, held[:, 2 * hidden :])
    terms_p, partial_r = after(terms_p, partial_r)
    terms_r = exchange(partial_r, "y")

    act_p, hid_p = halves(terms_p)
    summed_p = sum_of_shares(second(hid_p, down_of_p))
    diff_p = own(x_proxy) + summed_p - goal
    loss_p = jnp.mean(diff_p**2, axis=1)
    diff_low = diff_p.astype(BF16)

    terms_r, diff_low, loss_p, group = after(
        terms_r, diff_low, loss_p, jnp.where(alive, domain, NDOM)
    )
    _, hid_r = halves(terms_r)
    group = gather(group, "y")
    parts_r = exchange(second(hid_r, down_of_r), MP)
    parts_r, group = after(parts_r, group)
    diff_all = gather(diff_low, MP)
    diff_r = own(x_ref) + parts_r.astype(F32).sum(axis=0) - goal
    loss_r = jnp.mean(diff_r**2, axis=1)

    dhid = dot(diff_all, down_of_p, ((1,), (0,)))
    scaled = gather((dhid * act_p * (2.0 / width)).astype(BF16), "y")

    live_own = lax.dynamic_slice_in_dim(live, me * share, share, axis=0)
    domain_own = lax.dynamic_slice_in_dim(domain, me * share, share, axis=0)
    gained = live_own * jnp.maximum(loss_p - loss_r, 0.0)
    ids = jnp.arange(NDOM, dtype=jnp.int32)[None, :]
    onehot = (domain_own[:, None] == ids).astype(F32)
    sums = jnp.concatenate(
        [jnp.sum(onehot * gained[:, None], axis=0), jnp.sum(onehot * live_own[:, None], axis=0)]
    )
    sums = jnp.pad(sums, (0, LANES - 2 * NDOM))
    sums = share_all(sums, "z").sum(axis=0)
    sums = share_all(sums, ("y",) + MP).sum(axis=0)
    dsum, count = sums[:NDOM], sums[NDOM : 2 * NDOM]
    raw = prior_counts.astype(F32) * jnp.exp(1.0 * dsum / (count + 1.0))
    alpha = (1.0 - 0.001) * raw / jnp.sum(raw) + 0.001 / NDOM
    log_weights = jnp.log(alpha)
    table = alpha * total_rows / (count + 1.0)

    picks = (group[:, None] == ids).astype(F32)
    weight_tok = jnp.sum(picks * table[None, :], axis=1)
    dup = (scaled.astype(F32) * weight_tok[:, None]).astype(BF16)
    grad = dot(sliced_p, dup, ((0,), (0,))).astype(BF16)
    grad, gained = after(grad, gained)
    grad_up = exchange(grad.reshape(n_z, -1, hidden), "z").astype(F32).sum(axis=0)
    excess = gather(gained, MP)
    return (excess, log_weights, grad_up)


def solution(mesh):
    fine = Mesh(mesh.devices.reshape(4, 16, 4, 2), DP + MP)
    tokens, weights = P(DP, None), P(DP, MP)
    in_specs = (
        tokens,
        tokens,
        tokens,
        P(DP),
        P(DP),
        P(),
        weights,
        weights,
        P(MP, DP),
        weights,
        weights,
        P(MP, DP),
    )
    out_specs = (P(DP), P(), weights)
    return jax.shard_map(body, mesh=fine, in_specs=in_specs, out_specs=out_specs, check_vma=False)
```

```python
import jax
import jax.numpy as jnp
from jax import lax
from jax.sharding import Mesh
from jax.sharding import PartitionSpec as P

NDOM = 22
LANES = 128
BF16 = jnp.bfloat16
F32 = jnp.float32
DP = ("y", "z")
MP = ("x", "c")


def dot(a, b, dims):
    return lax.dot_general(a, b, (dims, ((), ())), preferred_element_type=F32)


def exchange(value, axis):
    return lax.all_to_all(value, axis, 0, 0, tiled=True)


def gather(value, axis):
    return lax.all_gather(value, axis, axis=0, tiled=True)


def share_all(value, axis):
    copies = jnp.broadcast_to(value[None], (lax.axis_size(axis),) + value.shape)
    return lax.all_to_all(copies, axis, 0, 0, tiled=True)


def sum_of_shares(shares):
    n_x, n_c = lax.axis_size("x"), lax.axis_size("c")
    x, c = lax.axis_index("x"), lax.axis_index("c")
    shares = shares.reshape((n_x, n_c) + shares.shape[1:])
    keep = lax.dynamic_index_in_dim(shares, c, 1, keepdims=False)
    give = lax.dynamic_index_in_dim(shares, (c + 1) % n_c, 1, keepdims=False)
    got = lax.ppermute(give, "c", [(i, (i + 1) % n_c) for i in range(n_c)])
    pair = keep.astype(F32) + got.astype(F32)
    low = pair.astype(BF16)
    total = lax.dynamic_index_in_dim(pair, x, 0, keepdims=False)
    for k in range(1, n_x):
        block = lax.dynamic_index_in_dim(low, (x + k) % n_x, 0, keepdims=False)
        perm = [(i, (i + k) % n_x) for i in range(n_x)]
        total = total + lax.ppermute(block, "x", perm).astype(F32)
    return total


def after(*values):
    return lax.optimization_barrier(values)


def column_parts(x, parts):
    rows, width = x.shape
    return x.reshape(rows, parts, width // parts).transpose(1, 0, 2)


def body(
    x_proxy,
    x_ref,
    target,
    domain,
    live_tokens,
    prior_counts,
    gate_p,
    up_p,
    down_p,
    gate_r,
    up_r,
    down_r,
):
    rows, width = x_proxy.shape
    hidden = gate_p.shape[1]
    n_y, n_z = lax.axis_size("y"), lax.axis_size("z")
    n_dp, n_mp = n_y * n_z, lax.axis_size(MP)
    total_rows = rows * n_dp
    share = rows // n_mp
    me = lax.axis_index(MP)

    slots = jnp.arange(rows, dtype=jnp.int32)
    alive = slots < live_tokens[0]
    live = alive.astype(F32)

    upper = jnp.concatenate([gate_p, up_p, gate_r, up_r], axis=1)
    upper, lower = after(upper, jnp.concatenate([down_p.T, down_r.T], axis=1))
    lower = gather(lower[None], "y").transpose(1, 0, 2).reshape(upper.shape[0], -1)
    packed = jnp.concatenate([upper, lower], axis=1)
    packed, whole_p, whole_r = after(packed, x_proxy, x_ref)
    held = gather(packed, "z")

    parts = jnp.stack([column_parts(whole_p, n_y), column_parts(whole_r, n_y)], axis=1)
    sliced = exchange(parts, "y")
    sliced_p = sliced[:, 0].reshape(n_y * rows, -1)
    sliced_r = sliced[:, 1].reshape(n_y * rows, -1)
    group = gather(after(jnp.where(alive, domain, NDOM), sliced)[0], "y")
    held, sliced_p, sliced_r, group = after(held, sliced_p, sliced_r, group)

    def whole_down(which):
        starts = [(4 + 2 * k + which) * hidden for k in range(n_y)]
        return jnp.concatenate([held[:, i : i + hidden] for i in starts], axis=0)

    down_of_p, down_of_r = whole_down(0), whole_down(1)

    def first(sliced, weights):
        partial = dot(sliced, weights, ((1,), (0,))).astype(BF16)
        return partial.reshape(n_y, rows, 2 * hidden)

    def halves(terms):
        both = terms.astype(F32).sum(axis=0)
        act = jax.nn.silu(both[:, :hidden])
        return act, (act * both[:, hidden:]).astype(BF16)

    def second(hid, down_w):
        part = dot(hid, down_w, ((1,), (1,))).astype(BF16)
        return part.reshape(n_mp, share, width)

    def own(x):
        return lax.dynamic_slice_in_dim(x, me * share, share, axis=0).astype(F32)

    goal = own(target)
    terms_p = exchange(first(sliced_p, held[:, : 2 * hidden]), "y")
    partial_r = first(sliced_r, held[:, 2 * hidden : 4 * hidden])
    terms_p, partial_r = after(terms_p, partial_r)
    terms_r = exchange(partial_r, "y")

    act_p, hid_p = halves(terms_p)
    summed_p = sum_of_shares(second(hid_p, down_of_p))
    diff_p = own(x_proxy) + summed_p - goal
    loss_p = jnp.mean(diff_p**2, axis=1)
    diff_low = diff_p.astype(BF16)

    terms_r, diff_low, loss_p = after(terms_r, diff_low, loss_p)
    _, hid_r = halves(terms_r)
    parts_r = exchange(second(hid_r, down_of_r), MP)
    diff_all = gather(diff_low, MP)
    diff_r = own(x_ref) + parts_r.astype(F32).sum(axis=0) - goal
    loss_r = jnp.mean(diff_r**2, axis=1)

    gained = jnp.maximum(loss_p - loss_r, 0.0)
    gained = share_all(jnp.pad(gained, (0, LANES - share)), MP)
    excess = live * gained[:, :share].reshape(rows)
    ids = jnp.arange(NDOM, dtype=jnp.int32)[None, :]
    onehot = (domain[:, None] == ids).astype(F32)
    sums = jnp.concatenate(
        [jnp.sum(onehot * excess[:, None], axis=0), jnp.sum(onehot * live[:, None], axis=0)]
    )
    sums = share_all(jnp.pad(sums, (0, LANES - 2 * NDOM)), DP).sum(axis=0)

    diff_all, _ = after(diff_all, gained)
    dhid = dot(diff_all, down_of_p, ((1,), (0,)))
    scaled = gather((dhid * act_p * (2.0 / width)).astype(BF16), "y")

    dsum, count = sums[:NDOM], sums[NDOM : 2 * NDOM]
    raw = prior_counts.astype(F32) * jnp.exp(1.0 * dsum / (count + 1.0))
    alpha = (1.0 - 0.001) * raw / jnp.sum(raw) + 0.001 / NDOM
    log_weights = jnp.log(alpha)
    table = alpha * total_rows / (count + 1.0)

    picks = (group[:, None] == ids).astype(F32)
    weight_tok = jnp.sum(picks * table[None, :], axis=1)
    dup = (scaled.astype(F32) * weight_tok[:, None]).astype(BF16)
    grad = dot(sliced_p, dup, ((0,), (0,))).astype(BF16)
    grad_up = exchange(grad.reshape(n_z, -1, hidden), "z").astype(F32).sum(axis=0)
    return (excess, log_weights, grad_up)


def solution(mesh):
    fine = Mesh(mesh.devices.reshape(4, 16, 4, 2), DP + MP)
    tokens, weights = P(DP, None), P(DP, MP)
    in_specs = (
        tokens,
        tokens,
        tokens,
        P(DP),
        P(DP),
        P(),
        weights,
        weights,
        P(MP, DP),
        weights,
        weights,
        P(MP, DP),
    )
    out_specs = (P(DP), P(), weights)
    return jax.shard_map(body, mesh=fine, in_specs=in_specs, out_specs=out_specs, check_vma=False)
```

```python
import jax
import jax.numpy as jnp
from jax import lax
from jax.sharding import Mesh
from jax.sharding import PartitionSpec as P

NDOM = 22
LANES = 128
BF16 = jnp.bfloat16
F32 = jnp.float32
DP = ("y", "z")
MP = ("x", "c")


def dot(a, b, dims):
    return lax.dot_general(a, b, (dims, ((), ())), preferred_element_type=F32)


def exchange(value, axis):
    return lax.all_to_all(value, axis, 0, 0, tiled=True)


def gather(value, axis):
    return lax.all_gather(value, axis, axis=0, tiled=True)


def share_all(value, axis):
    copies = jnp.broadcast_to(value[None], (lax.axis_size(axis),) + value.shape)
    return lax.all_to_all(copies, axis, 0, 0, tiled=True)


def sum_of_shares(shares):
    n_x, n_c = lax.axis_size("x"), lax.axis_size("c")
    x, c = lax.axis_index("x"), lax.axis_index("c")
    shares = shares.reshape((n_x, n_c) + shares.shape[1:])
    keep = lax.dynamic_index_in_dim(shares, c, 1, keepdims=False)
    give = lax.dynamic_index_in_dim(shares, (c + 1) % n_c, 1, keepdims=False)
    got = lax.ppermute(give, "c", [(i, (i + 1) % n_c) for i in range(n_c)])
    pair = keep.astype(F32) + got.astype(F32)
    low = pair.astype(BF16)
    total = lax.dynamic_index_in_dim(pair, x, 0, keepdims=False)
    for k in range(1, n_x):
        block = lax.dynamic_index_in_dim(low, (x + k) % n_x, 0, keepdims=False)
        perm = [(i, (i + k) % n_x) for i in range(n_x)]
        total = total + lax.ppermute(block, "x", perm).astype(F32)
    return total


def after(*values):
    return lax.optimization_barrier(values)


def column_parts(x, parts):
    rows, width = x.shape
    return x.reshape(rows, parts, width // parts).transpose(1, 0, 2)


def body(
    x_proxy,
    x_ref,
    target,
    domain,
    live_tokens,
    prior_counts,
    gate_p,
    up_p,
    down_p,
    gate_r,
    up_r,
    down_r,
):
    rows, width = x_proxy.shape
    hidden = gate_p.shape[1]
    n_y, n_z = lax.axis_size("y"), lax.axis_size("z")
    n_dp, n_mp = n_y * n_z, lax.axis_size(MP)
    total_rows = rows * n_dp
    share = rows // n_mp
    me = lax.axis_index(MP)

    packed, lower = after(jnp.concatenate([gate_p, up_p, gate_r, up_r], axis=1), down_r.T)
    packed = jnp.concatenate([packed, lower], axis=1)
    packed, whole_p, whole_r = after(packed, x_proxy, x_ref)
    held = gather(packed, "z")

    parts = jnp.stack([column_parts(whole_p, n_y), column_parts(whole_r, n_y)], axis=1)
    sliced = exchange(parts, "y")
    sliced_p = sliced[:, 0].reshape(n_y * rows, -1)
    sliced_r = sliced[:, 1].reshape(n_y * rows, -1)

    slots = jnp.arange(rows, dtype=jnp.int32)
    alive = slots < live_tokens[0]
    live = alive.astype(F32)
    down_of_p = share_all(gather(down_p.T, "z"), "y").reshape(width, hidden)
    held, sliced_p, sliced_r, down_of_p = after(held, sliced_p, sliced_r, down_of_p)
    down_of_r = gather(held[:, 4 * hidden :], "y")

    def first(sliced, weights):
        partial = dot(sliced, weights, ((1,), (0,))).astype(BF16)
        return partial.reshape(n_y, rows, 2 * hidden)

    def halves(terms):
        both = terms.astype(F32).sum(axis=0)
        act = jax.nn.silu(both[:, :hidden])
        return act, (act * both[:, hidden:]).astype(BF16)

    def second(hid, down_w):
        part = dot(hid, down_w, ((1,), (1,))).astype(BF16)
        return part.reshape(n_mp, share, width)

    def own(x):
        return lax.dynamic_slice_in_dim(x, me * share, share, axis=0).astype(F32)

    goal = own(target)
    terms_p = exchange(first(sliced_p, held[:, : 2 * hidden]), "y")
    partial_r = first(sliced_r, held[:, 2 * hidden : 4 * hidden])
    terms_p, partial_r = after(terms_p, partial_r)
    terms_r = exchange(partial_r, "y")

    act_p, hid_p = halves(terms_p)
    summed_p = sum_of_shares(second(hid_p, down_of_p))
    diff_p = own(x_proxy) + summed_p - goal
    loss_p = jnp.mean(diff_p**2, axis=1)
    diff_low = diff_p.astype(BF16)
    diff_all = gather(diff_low, MP)

    terms_r, diff_low, loss_p, group = after(
        terms_r, diff_low, loss_p, jnp.where(alive, domain, NDOM)
    )
    _, hid_r = halves(terms_r)
    group = gather(group, "y")
    parts_r = exchange(second(hid_r, down_of_r), MP)
    dhid = dot(diff_all, down_of_p, ((1,), (0,)))
    plain = (dhid * act_p * (2.0 / width)).astype(BF16)
    scaled = gather(plain, "y")
    parts_r, group, _ = after(parts_r, group, plain)
    diff_r = own(x_ref) + parts_r.astype(F32).sum(axis=0) - goal
    loss_r = jnp.mean(diff_r**2, axis=1)

    live_own = lax.dynamic_slice_in_dim(live, me * share, share, axis=0)
    domain_own = lax.dynamic_slice_in_dim(domain, me * share, share, axis=0)
    gained = live_own * jnp.maximum(loss_p - loss_r, 0.0)
    ids = jnp.arange(NDOM, dtype=jnp.int32)[None, :]
    onehot = (domain_own[:, None] == ids).astype(F32)
    sums = jnp.concatenate(
        [jnp.sum(onehot * gained[:, None], axis=0), jnp.sum(onehot * live_own[:, None], axis=0)]
    )
    sums = jnp.pad(sums, (0, LANES - 2 * NDOM))
    sums = share_all(sums, "z").sum(axis=0)
    sums = share_all(sums, ("y",) + MP).sum(axis=0)
    dsum, count = sums[:NDOM], sums[NDOM : 2 * NDOM]
    raw = prior_counts.astype(F32) * jnp.exp(1.0 * dsum / (count + 1.0))
    alpha = (1.0 - 0.001) * raw / jnp.sum(raw) + 0.001 / NDOM
    log_weights = jnp.log(alpha)
    table = alpha * total_rows / (count + 1.0)

    picks = (group[:, None] == ids).astype(F32)
    weight_tok = jnp.sum(picks * table[None, :], axis=1)
    dup = (scaled.astype(F32) * weight_tok[:, None]).astype(BF16)
    grad = dot(sliced_p, dup, ((0,), (0,))).astype(BF16)
    grad, gained = after(grad, gained)
    grad_up = exchange(grad.reshape(n_z, -1, hidden), "z").astype(F32).sum(axis=0)
    excess = gather(gained, MP)
    return (excess, log_weights, grad_up)


def solution(mesh):
    fine = Mesh(mesh.devices.reshape(4, 16, 4, 2), DP + MP)
    tokens, weights = P(DP, None), P(DP, MP)
    in_specs = (
        tokens,
        tokens,
        tokens,
        P(DP),
        P(DP),
        P(),
        weights,
        weights,
        P(MP, DP),
        weights,
        weights,
        P(MP, DP),
    )
    out_specs = (P(DP), P(), weights)
    return jax.shard_map(body, mesh=fine, in_specs=in_specs, out_specs=out_specs, check_vma=False)
```

```python
import jax
import jax.numpy as jnp
from jax import lax
from jax.sharding import Mesh
from jax.sharding import PartitionSpec as P

NDOM = 22
LANES = 128
BF16 = jnp.bfloat16
F32 = jnp.float32
DP = ("y", "z")
MP = ("x", "c")


def dot(a, b, dims):
    return lax.dot_general(a, b, (dims, ((), ())), preferred_element_type=F32)


def exchange(value, axis):
    return lax.all_to_all(value, axis, 0, 0, tiled=True)


def gather(value, axis):
    return lax.all_gather(value, axis, axis=0, tiled=True)


def share_all(value, axis):
    copies = jnp.broadcast_to(value[None], (lax.axis_size(axis),) + value.shape)
    return lax.all_to_all(copies, axis, 0, 0, tiled=True)


def sum_of_shares(shares):
    n_x, n_c = lax.axis_size("x"), lax.axis_size("c")
    x, c = lax.axis_index("x"), lax.axis_index("c")
    shares = shares.reshape((n_x, n_c) + shares.shape[1:])
    keep = lax.dynamic_index_in_dim(shares, c, 1, keepdims=False)
    give = lax.dynamic_index_in_dim(shares, (c + 1) % n_c, 1, keepdims=False)
    got = lax.ppermute(give, "c", [(i, (i + 1) % n_c) for i in range(n_c)])
    pair = keep.astype(F32) + got.astype(F32)
    low = pair.astype(BF16)
    total = lax.dynamic_index_in_dim(pair, x, 0, keepdims=False)
    for k in range(1, n_x):
        block = lax.dynamic_index_in_dim(low, (x + k) % n_x, 0, keepdims=False)
        perm = [(i, (i + k) % n_x) for i in range(n_x)]
        total = total + lax.ppermute(block, "x", perm).astype(F32)
    return total


def after(*values):
    return lax.optimization_barrier(values)


def column_parts(x, parts):
    rows, width = x.shape
    return x.reshape(rows, parts, width // parts).transpose(1, 0, 2)


def body(
    x_proxy,
    x_ref,
    target,
    domain,
    live_tokens,
    prior_counts,
    gate_p,
    up_p,
    down_p,
    gate_r,
    up_r,
    down_r,
):
    rows, width = x_proxy.shape
    hidden = gate_p.shape[1]
    n_y, n_z = lax.axis_size("y"), lax.axis_size("z")
    n_dp, n_mp = n_y * n_z, lax.axis_size(MP)
    total_rows = rows * n_dp
    share = rows // n_mp
    me = lax.axis_index(MP)

    packed, lower = after(jnp.concatenate([gate_p, up_p, gate_r, up_r], axis=1), down_r.T)
    packed = jnp.concatenate([packed, lower], axis=1)
    packed, whole_p, whole_r = after(packed, x_proxy, x_ref)
    held = gather(packed, "z")

    parts = jnp.stack([column_parts(whole_p, n_y), column_parts(whole_r, n_y)], axis=1)
    sliced = exchange(parts, "y")
    sliced_p = sliced[:, 0].reshape(n_y * rows, -1)
    sliced_r = sliced[:, 1].reshape(n_y * rows, -1)

    slots = jnp.arange(rows, dtype=jnp.int32)
    alive = slots < live_tokens[0]
    live = alive.astype(F32)
    down_of_p = share_all(gather(down_p.T, "z"), "y").reshape(width, hidden)
    held, sliced_p, sliced_r, down_of_p = after(held, sliced_p, sliced_r, down_of_p)
    down_of_r = gather(held[:, 4 * hidden :], "y")

    def first(sliced, weights):
        partial = dot(sliced, weights, ((1,), (0,))).astype(BF16)
        return partial.reshape(n_y, rows, 2 * hidden)

    def halves(terms):
        both = terms.astype(F32).sum(axis=0)
        act = jax.nn.silu(both[:, :hidden])
        return act, (act * both[:, hidden:]).astype(BF16)

    def second(hid, down_w):
        part = dot(hid, down_w, ((1,), (1,))).astype(BF16)
        return part.reshape(n_mp, share, width)

    def own(x):
        return lax.dynamic_slice_in_dim(x, me * share, share, axis=0).astype(F32)

    goal = own(target)
    terms_p = exchange(first(sliced_p, held[:, : 2 * hidden]), "y")
    partial_r = first(sliced_r, held[:, 2 * hidden : 4 * hidden])
    terms_p, partial_r = after(terms_p, partial_r)
    terms_r = exchange(partial_r, "y")

    act_p, hid_p = halves(terms_p)
    summed_p = sum_of_shares(second(hid_p, down_of_p))
    diff_p = own(x_proxy) + summed_p - goal
    loss_p = jnp.mean(diff_p**2, axis=1)
    diff_low = diff_p.astype(BF16)
    diff_all = gather(diff_low, MP)

    terms_r, diff_low, loss_p, group = after(
        terms_r, diff_low, loss_p, jnp.where(alive, domain, NDOM)
    )
    _, hid_r = halves(terms_r)
    group = gather(group, "y")
    parts_r = exchange(second(hid_r, down_of_r), MP)
    dhid = dot(diff_all, down_of_p, ((1,), (0,)))
    plain = (dhid * act_p * (2.0 / width)).astype(BF16)
    scaled = gather(plain, "y")
    parts_r, group, _ = after(parts_r, group, plain)
    diff_r = own(x_ref) + parts_r.astype(F32).sum(axis=0) - goal
    loss_r = jnp.mean(diff_r**2, axis=1)

    live_own = lax.dynamic_slice_in_dim(live, me * share, share, axis=0)
    domain_own = lax.dynamic_slice_in_dim(domain, me * share, share, axis=0)
    gained = live_own * jnp.maximum(loss_p - loss_r, 0.0)
    ids = jnp.arange(NDOM, dtype=jnp.int32)[None, :]
    onehot = (domain_own[:, None] == ids).astype(F32)
    sums = jnp.concatenate(
        [jnp.sum(onehot * gained[:, None], axis=0), jnp.sum(onehot * live_own[:, None], axis=0)]
    )
    sums = jnp.pad(sums, (0, LANES - 2 * NDOM))
    sums = share_all(sums, DP).sum(axis=0)
    sums = share_all(sums, MP).sum(axis=0)
    dsum, count = sums[:NDOM], sums[NDOM : 2 * NDOM]
    raw = prior_counts.astype(F32) * jnp.exp(1.0 * dsum / (count + 1.0))
    alpha = (1.0 - 0.001) * raw / jnp.sum(raw) + 0.001 / NDOM
    log_weights = jnp.log(alpha)
    table = alpha * total_rows / (count + 1.0)

    picks = (group[:, None] == ids).astype(F32)
    weight_tok = jnp.sum(picks * table[None, :], axis=1)
    dup = (scaled.astype(F32) * weight_tok[:, None]).astype(BF16)
    grad = dot(sliced_p, dup, ((0,), (0,))).astype(BF16)
    grad, gained = after(grad, gained)
    grad_up = exchange(grad.reshape(n_z, -1, hidden), "z").astype(F32).sum(axis=0)
    excess = gather(gained, MP)
    return (excess, log_weights, grad_up)


def solution(mesh):
    fine = Mesh(mesh.devices.reshape(4, 16, 4, 2), DP + MP)
    tokens, weights = P(DP, None), P(DP, MP)
    in_specs = (
        tokens,
        tokens,
        tokens,
        P(DP),
        P(DP),
        P(),
        weights,
        weights,
        P(MP, DP),
        weights,
        weights,
        P(MP, DP),
    )
    out_specs = (P(DP), P(), weights)
    return jax.shard_map(body, mesh=fine, in_specs=in_specs, out_specs=out_specs, check_vma=False)
```

```python
import jax
import jax.numpy as jnp
from jax import lax
from jax.sharding import Mesh
from jax.sharding import PartitionSpec as P

NDOM = 22
LANES = 128
BF16 = jnp.bfloat16
F32 = jnp.float32
DP = ("y", "z")
MP = ("x", "c")


def dot(a, b, dims):
    return lax.dot_general(a, b, (dims, ((), ())), preferred_element_type=F32)


def exchange(value, axis):
    return lax.all_to_all(value, axis, 0, 0, tiled=True)


def gather(value, axis):
    return lax.all_gather(value, axis, axis=0, tiled=True)


def share_all(value, axis):
    copies = jnp.broadcast_to(value[None], (lax.axis_size(axis),) + value.shape)
    return lax.all_to_all(copies, axis, 0, 0, tiled=True)


def sent_blocks(blocks, axis):
    n, i = lax.axis_size(axis), lax.axis_index(axis)
    terms = [lax.dynamic_index_in_dim(blocks, i, 0, keepdims=False)]
    for k in range(1, n):
        block = lax.dynamic_index_in_dim(blocks, (i + k) % n, 0, keepdims=False)
        terms.append(lax.ppermute(block, axis, [(j, (j + k) % n) for j in range(n)]))
    return terms


def after(*values):
    return lax.optimization_barrier(values)


def column_parts(x, parts):
    rows, width = x.shape
    return x.reshape(rows, parts, width // parts).transpose(1, 0, 2)


def body(
    x_proxy,
    x_ref,
    target,
    domain,
    live_tokens,
    prior_counts,
    gate_p,
    up_p,
    down_p,
    gate_r,
    up_r,
    down_r,
):
    rows, width = x_proxy.shape
    hidden = gate_p.shape[1]
    n_y, n_z = lax.axis_size("y"), lax.axis_size("z")
    n_dp, n_mp = n_y * n_z, lax.axis_size(MP)
    total_rows = rows * n_dp
    share = rows // n_mp
    me = lax.axis_index(MP)

    packed, lower = after(jnp.concatenate([gate_p, up_p, gate_r, up_r], axis=1), down_r.T)
    packed = jnp.concatenate([packed, lower], axis=1)
    packed, whole_p, whole_r = after(packed, x_proxy, x_ref)
    held = gather(packed, "z")

    parts = jnp.stack([column_parts(whole_p, n_y), column_parts(whole_r, n_y)], axis=1)
    sliced = exchange(parts, "y")
    sliced_p = sliced[:, 0].reshape(n_y * rows, -1)
    sliced_r = sliced[:, 1].reshape(n_y * rows, -1)

    slots = jnp.arange(rows, dtype=jnp.int32)
    alive = slots < live_tokens[0]
    live = alive.astype(F32)
    down_of_p = share_all(gather(down_p.T, "z"), "y").reshape(width, hidden)
    held, sliced_p, sliced_r, down_of_p = after(held, sliced_p, sliced_r, down_of_p)
    down_of_r = gather(held[:, 4 * hidden :], "y")

    def first(sliced, weights):
        partial = dot(sliced, weights, ((1,), (0,))).astype(BF16)
        return partial.reshape(n_y, rows, 2 * hidden)

    def halves(both):
        act = jax.nn.silu(both[:, :hidden])
        return act, (act * both[:, hidden:]).astype(BF16)

    def second(hid, down_w):
        part = dot(hid, down_w, ((1,), (1,))).astype(BF16)
        return part.reshape(n_mp, share, width)

    def own(x):
        return lax.dynamic_slice_in_dim(x, me * share, share, axis=0).astype(F32)

    goal = own(target)
    terms_p = exchange(first(sliced_p, held[:, : 2 * hidden]), "y")
    terms_r = sent_blocks(first(sliced_r, held[:, 2 * hidden : 4 * hidden]), "y")

    terms_p, _ = after(terms_p, terms_r[1])
    act_p, hid_p = halves(terms_p.astype(F32).sum(axis=0))
    part_p, _ = after(second(hid_p, down_of_p), terms_r[3])
    parts_p, _ = after(exchange(part_p, MP), terms_r[2])
    both_r = sum(term.astype(F32) for term in terms_r)
    summed_p = parts_p.astype(F32).sum(axis=0)
    diff_p = own(x_proxy) + summed_p - goal
    loss_p = jnp.mean(diff_p**2, axis=1)
    diff_low = diff_p.astype(BF16)
    diff_all = gather(diff_low, MP)

    both_r, group, _ = after(both_r, jnp.where(alive, domain, NDOM), part_p)
    _, hid_r = halves(both_r)
    group = gather(group, "y")
    parts_r = exchange(second(hid_r, down_of_r), MP)
    dhid = dot(diff_all, down_of_p, ((1,), (0,)))
    plain = (dhid * act_p * (2.0 / width)).astype(BF16)
    scaled = gather(plain, "y")
    parts_r, group, _ = after(parts_r, group, plain)
    diff_r = own(x_ref) + parts_r.astype(F32).sum(axis=0) - goal
    loss_r = jnp.mean(diff_r**2, axis=1)

    live_own = lax.dynamic_slice_in_dim(live, me * share, share, axis=0)
    domain_own = lax.dynamic_slice_in_dim(domain, me * share, share, axis=0)
    gained = live_own * jnp.maximum(loss_p - loss_r, 0.0)
    ids = jnp.arange(NDOM, dtype=jnp.int32)[None, :]
    onehot = (domain_own[:, None] == ids).astype(F32)
    sums = jnp.concatenate(
        [jnp.sum(onehot * gained[:, None], axis=0), jnp.sum(onehot * live_own[:, None], axis=0)]
    )
    sums = jnp.pad(sums, (0, LANES - 2 * NDOM))
    sums = share_all(sums, DP).sum(axis=0)
    sums = share_all(sums, MP).sum(axis=0)
    dsum, count = sums[:NDOM], sums[NDOM : 2 * NDOM]
    raw = prior_counts.astype(F32) * jnp.exp(1.0 * dsum / (count + 1.0))
    alpha = (1.0 - 0.001) * raw / jnp.sum(raw) + 0.001 / NDOM
    log_weights = jnp.log(alpha)
    table = alpha * total_rows / (count + 1.0)

    picks = (group[:, None] == ids).astype(F32)
    weight_tok = jnp.sum(picks * table[None, :], axis=1)
    dup = (scaled.astype(F32) * weight_tok[:, None]).astype(BF16)
    grad = dot(sliced_p, dup, ((0,), (0,))).astype(BF16)
    grad, gained = after(grad, gained)
    grad_up = exchange(grad.reshape(n_z, -1, hidden), "z").astype(F32).sum(axis=0)
    excess = gather(gained, MP)
    return (excess, log_weights, grad_up)


def solution(mesh):
    fine = Mesh(mesh.devices.reshape(4, 16, 4, 2), DP + MP)
    tokens, weights = P(DP, None), P(DP, MP)
    in_specs = (
        tokens,
        tokens,
        tokens,
        P(DP),
        P(DP),
        P(),
        weights,
        weights,
        P(MP, DP),
        weights,
        weights,
        P(MP, DP),
    )
    out_specs = (P(DP), P(), weights)
    return jax.shard_map(body, mesh=fine, in_specs=in_specs, out_specs=out_specs, check_vma=False)
```
